32 devices in a mesh: grp: 2 (over x), ctx: 16 (over z, y, core).
Axes of the slice: x: 2, y: 2, z: 4, core: 2. Of those that a mesh axis runs over, the one named last changes fastest.
Arguments:
- queries: bfloat16 [16384, 2048], P(('grp', 'ctx')), parts along dimension 0, may hold values from -7 to 7
- keys: bfloat16 [16384, 512], P(('grp', 'ctx')), parts along dimension 0, may hold values from -6 to 6
- values: bfloat16 [16384, 512], P(('grp', 'ctx')), parts along dimension 0, may hold values from -6 to 6
- out_grad: bfloat16 [16384, 2048], P(('grp', 'ctx')), parts along dimension 0, may hold values from -6 to 6
- doc_starts: int32 [16], P('grp'), parts along dimension 0, may hold values from 0 to 7423, as said below
- block_lists: int32 [128, 6], P(('grp', 'ctx')), parts along dimension 0, may hold values from -1 to 63, as said below
Outputs:
- attended: bfloat16 [16384, 2048], P(('grp', 'ctx')), parts along dimension 0
- grad_queries: bfloat16 [16384, 2048], P(('grp', 'ctx')), parts along dimension 0
- grad_keys: bfloat16 [16384, 512], P(('grp', 'ctx')), parts along dimension 0
- grad_values: bfloat16 [16384, 512], P(('grp', 'ctx')), parts along dimension 0
The draws below stay inside these ranges and needn't reach their ends.
There are 2 independent parts, one for each index of `grp`. The reference program is written for one: setup_inputs(seed, part) draws one part's arguments, and reference() takes and returns one part's arrays. A program takes and returns all parts, laid end to end along the dimension named above; each array names one. Nothing has to cross between parts.
Inputs may be any that keep to these rules, and one draw needn't show every extreme that they name: `block_lists`: row b lists block b first, then further distinct blocks before b that lie in the document of b's last token and among the blocks of b's device or of the 2 devices before it, then -1 in every slot left empty; the last row is full. `doc_starts`: Increasing, the first entry 0.
All inputs are finite; a program needn't handle non-finite values.
Results may differ from the reference program's by a relative error of at most 0.029.
Values may be sent and summed in bfloat16 or wider, within the bound.
A program may use at most 128 MiB of HBM per device.

```python
import jax
import jax.numpy as jnp
from jax import lax

HD = 128
HEADS = 16
KV_HEADS = 4
BLOCK = 128
BLK_DEV = 4
LIST = 6
R_DEV = 2
DOCS = 8
SEQ = 8192
NBLK = 64


def doc_and_lists(key):
    base = jax.random.fold_in(key, 101)
    start_key, score_key, count_key = jax.random.split(base, 3)
    span = SEQ // DOCS
    shake = span // 4
    order = jnp.arange(DOCS, dtype=jnp.int32)
    jitter = jax.random.randint(start_key, (DOCS,), -shake, shake)
    starts = jnp.where(order == 0, 0, order * span + jitter).astype(jnp.int32)
    blocks_all = jnp.arange(NBLK, dtype=jnp.int32)
    last_token = blocks_all * BLOCK + BLOCK - 1
    doc_last = jnp.sum((last_token[:, None] >= starts[None, 1:]).astype(jnp.int32), axis=1)
    doc_first = jnp.sum(jnp.where(doc_last[:, None] == order[None, :], starts[None, :], 0), axis=1)
    lowest = jnp.maximum(doc_first // BLOCK, (blocks_all // BLK_DEV - R_DEV) * BLK_DEV)
    lowest = jnp.maximum(lowest, 0)
    available = blocks_all - lowest + 1
    wanted = jax.random.randint(count_key, (NBLK,), 2, LIST + 1)
    live_count = jnp.minimum(available, wanted)
    live_count = jnp.where(blocks_all == NBLK - 1, jnp.minimum(available, LIST), live_count)
    reach_back = (R_DEV + 1) * BLK_DEV - 1
    backward = jnp.arange(1, reach_back + 1, dtype=jnp.int32)
    candidates = blocks_all[:, None] - backward[None, :]
    noise = jax.random.randint(score_key, (NBLK, reach_back), 0, 65536)
    ranking = jnp.where(candidates >= lowest[:, None], noise * 64 + backward[None, :], -1 - backward[None, :])
    top_values, top_index = lax.top_k(ranking, LIST - 1)
    chosen = blocks_all[:, None] - (top_index.astype(jnp.int32) + 1)
    slot_ids = jnp.arange(1, LIST, dtype=jnp.int32)
    remaining = jnp.where(slot_ids[None, :] < live_count[:, None], chosen, -1)
    lists = jnp.concatenate([blocks_all[:, None], remaining], axis=1).astype(jnp.int32)
    return (starts, lists)


def draw_doc_starts(key, part):
    return doc_and_lists(key)[0]


def draw_block_lists(key, part):
    return doc_and_lists(key)[1]


def drawn_pair(key):
    base = jax.random.fold_in(key, 202)
    query_key, key_key = jax.random.split(base, 2)
    queries = jnp.clip(jax.random.normal(query_key, (SEQ, HEADS * HD), jnp.float32), -6.0, 6.0)
    keys = jnp.clip(jax.random.normal(key_key, (SEQ, KV_HEADS * HD), jnp.float32), -6.0, 6.0)
    return (queries, keys)


def draw_queries(key, part):
    return drawn_pair(key)[0].astype(jnp.bfloat16)


def draw_keys(key, part):
    return drawn_pair(key)[1].astype(jnp.bfloat16)


def steps_of(rng, shape, pieces, least, high):
    def one(axis_at, blocks):
        heights = jax.random.uniform(jax.random.fold_in(jax.random.fold_in(rng, 6), axis_at), (blocks,), jnp.float32, least / len(pieces), high / len(pieces))
        return jnp.repeat(jnp.exp(heights), shape[axis_at] // blocks).reshape((-1,) + (1,) * (len(shape) - axis_at - 1))

    gain = one(*pieces[0])
    for cut in pieces[1:]:
        gain = gain * one(*cut)
    return gain


def bell_draw(rng, shape, scale, most, cuts=(), kind=jnp.bfloat16):
    values = scale * jax.random.normal(rng, shape, jnp.float32)
    if cuts:
        values = values * steps_of(rng, shape, cuts, -0.22, 0.18)
    return jnp.clip(values, -most, most).astype(kind)


def setup_inputs(seed: int = 0, part: int = 0) -> dict:
    key_of = jax.random.split(jax.random.key(seed), 7)
    own_keys = jax.random.split(jax.random.fold_in(key_of[6], part), 7)
    return {
        "queries": draw_queries(jax.random.fold_in(jax.random.fold_in(key_of[6], part), 71), part),
        "keys": draw_keys(jax.random.fold_in(jax.random.fold_in(key_of[6], part), 71), part),
        "values": bell_draw(own_keys[2], (SEQ, KV_HEADS * HD), 1.0, 6.0, ((0, 16),)),
        "out_grad": bell_draw(own_keys[3], (SEQ, HEADS * HD), 1.0, 6.0, ((0, 16),)),
        "doc_starts": draw_doc_starts(jax.random.fold_in(jax.random.fold_in(key_of[6], part), 71), part),
        "block_lists": draw_block_lists(jax.random.fold_in(jax.random.fold_in(key_of[6], part), 71), part),
    }


def doc_index(positions, doc_starts):
    return jnp.sum((positions[..., None] >= doc_starts[1:]).astype(jnp.int32), axis=-1)


def reference(queries, keys, values, out_grad, doc_starts, block_lists):
    groups = HEADS // KV_HEADS
    scaling = HD ** -0.5
    key_blocks = keys.reshape(NBLK, BLOCK, KV_HEADS, HD)
    value_blocks = values.reshape(NBLK, BLOCK, KV_HEADS, HD)
    query_blocks = queries.reshape(NBLK, BLOCK, KV_HEADS, groups, HD)
    grad_blocks = out_grad.reshape(NBLK, BLOCK, KV_HEADS, groups, HD)
    offsets = jnp.arange(BLOCK, dtype=jnp.int32)

    def per_block(carried, inputs):
        acc_keys, acc_values = carried
        query_blk, grad_blk, entries, block_index = inputs
        listed = entries >= 0
        clamped = jnp.where(listed, entries, 0).astype(jnp.int32)
        key_tiles = key_blocks[clamped].astype(jnp.float32)
        value_tiles = value_blocks[clamped].astype(jnp.float32)
        query_full = query_blk.astype(jnp.float32)
        grad_full = grad_blk.astype(jnp.float32)
        query_pos = block_index * BLOCK + offsets
        key_pos = clamped[:, None] * BLOCK + offsets[None, :]
        same_doc = doc_index(key_pos, doc_starts)[None] == doc_index(query_pos, doc_starts)[:, None, None]
        causal = key_pos[None] <= query_pos[:, None, None]
        allowed = listed[None, :, None] & causal & same_doc
        scores = jnp.einsum('qgjd,lkgd->gjqlk', query_full, key_tiles) * scaling
        masked = jnp.where(allowed, scores, -1e30)
        row_max = jnp.max(masked, axis=(3, 4), keepdims=True)
        unnormed = jnp.where(allowed, jnp.exp(masked - row_max), 0.0)
        attn_probs = unnormed / jnp.sum(unnormed, axis=(3, 4), keepdims=True)
        probs_low = attn_probs.astype(jnp.bfloat16)
        probs_full = probs_low.astype(jnp.float32)
        attended = jnp.einsum('gjqlk,lkgd->qgjd', probs_full, value_tiles).astype(jnp.bfloat16)
        row_delta = jnp.einsum('qgjd,qgjd->gjq', grad_full, attended.astype(jnp.float32))
        dprobs = jnp.einsum('qgjd,lkgd->gjqlk', grad_full, value_tiles)
        grad_scores = (attn_probs * (dprobs - row_delta[..., None, None])).astype(jnp.bfloat16)
        scores_full = grad_scores.astype(jnp.float32)
        grad_query = (jnp.einsum('gjqlk,lkgd->qgjd', scores_full, key_tiles) * scaling).astype(jnp.bfloat16)
        grad_key_tiles = jnp.einsum('gjqlk,qgjd->lkgd', scores_full, query_full) * scaling
        grad_value_tiles = jnp.einsum('gjqlk,qgjd->lkgd', probs_full, grad_full)
        acc_keys = acc_keys.at[clamped].add(grad_key_tiles)
        acc_values = acc_values.at[clamped].add(grad_value_tiles)
        return (acc_keys, acc_values), (attended, grad_query)

    zeros_acc = jnp.zeros((NBLK, BLOCK, KV_HEADS, HD), jnp.float32)
    indices = jnp.arange(NBLK, dtype=jnp.int32)
    (acc_keys, acc_values), (attended, grad_query) = lax.scan(
        per_block, (zeros_acc, zeros_acc), (query_blocks, grad_blocks, block_lists, indices))
    return (attended.reshape(SEQ, HEADS * HD),
            grad_query.reshape(SEQ, HEADS * HD),
            acc_keys.astype(jnp.bfloat16).reshape(SEQ, KV_HEADS * HD),
            acc_values.astype(jnp.bfloat16).reshape(SEQ, KV_HEADS * HD))
```

```python
import functools

import jax
import jax.numpy as jnp
from jax import lax
from jax.experimental import pallas as pl
from jax.experimental.pallas import tpu as pltpu
from jax.sharding import PartitionSpec as P

HD = 128
BLOCK = 128
R_DEV = 2
MESH = pl.DeviceIdType.MESH
FAR = 1 << 30


def kernel(
    n, blocks, slots, kv_heads, groups,
    index_ref, base_ref, inverse_ref, starts_ref, key_hbm, value_hbm, query_ref, grad_ref,
    out_ref, dquery_ref, dkey_ref, dvalue_ref,
    window, current, turned, bias, parts, own, send_a, send_b, take_a, take_b,
    local_sem, a_send, a_recv, b_send, b_recv, ga_send, ga_recv, gb_send, gb_recv,
):
    me = lax.axis_index("ctx")
    odd = lax.rem(me, 2) == 1
    even = jnp.logical_not(odd)
    partner = me + 1 - 2 * lax.rem(me, 2)
    ahead = lax.rem(me + 2, n)
    behind = lax.rem(me + n - 2, n)
    here = pl.ds(2 * blocks, blocks)
    near = pl.ds(blocks, blocks)
    far = pl.ds(0, blocks)
    span = slots * BLOCK
    scaling = HD ** (-0.5)
    scale2 = scaling * 1.4426950408889634

    def local_copies(g):
        cols = pl.ds(pl.multiple_of(g * HD, HD), HD)
        return [
            pltpu.make_async_copy(
                ref.at[:, :, cols], window.at[g, kind, here], local_sem.at[g, kind]
            )
            for kind, ref in enumerate((key_hbm, value_hbm))
        ]

    def remote(src, dst, send, recv, target):
        return pltpu.make_async_remote_copy(
            src_ref=src, dst_ref=dst, send_sem=send, recv_sem=recv,
            device_id={"ctx": target}, device_id_type=MESH,
        )

    def copy_a(g):
        return remote(
            window.at[g, :, here], window.at[g, :, far], a_send.at[g], a_recv.at[g], ahead
        )

    def copy_b(g, source):
        return remote(
            window.at[g, :, source], window.at[g, :, near], b_send.at[g], b_recv.at[g], partner
        )

    def grad_a(g):
        return remote(send_a.at[g], take_a.at[g], ga_send.at[g], ga_recv.at[g], behind)

    def grad_b(g):
        return remote(send_b.at[g], take_b.at[g], gb_send.at[g], gb_recv.at[g], partner)

    barrier = pltpu.get_barrier_semaphore()
    for other in (ahead, behind, partner):
        pl.semaphore_signal(barrier, inc=1, device_id={"ctx": other}, device_id_type=MESH)
    for g in range(kv_heads):
        for copy in local_copies(g):
            copy.start()
    pl.semaphore_wait(barrier, 3)
    for g in range(kv_heads):
        for copy in local_copies(g):
            copy.wait()
        copy_a(g).start()

        @pl.when(even)
        def _():
            copy_b(g, here).start()

    parts[:, blocks * slots] = jnp.zeros((2, BLOCK, HD), jnp.float32)
    first = me * (blocks * BLOCK)
    lanes = lax.broadcasted_iota(jnp.int32, (1, BLOCK), 1)
    rows = lax.broadcasted_iota(jnp.int32, (BLOCK, BLOCK), 0)
    for b in range(blocks):
        pos = first + b * BLOCK + lanes
        low = jnp.zeros_like(pos)
        for d in range(starts_ref.shape[0]):
            start = starts_ref[d]
            low = jnp.maximum(low, jnp.where(start <= pos, start, 0))
        for s in range(slots):
            at = base_ref[b, s] + rows
            keep = jnp.logical_and(at <= pos, at >= low)
            bias[b, pl.ds(s * BLOCK, BLOCK), :] = jnp.where(keep, 0.0, -1e30)

    def arrive(g):
        copy_a(g).wait_recv()

        @pl.when(odd)
        def _():
            copy_b(g, far).start()

    def forward_grad(g):
        grad_b(g).wait_recv()
        send_a[g] = (
            send_a[g].astype(jnp.float32) + take_b[g].astype(jnp.float32)
        ).astype(jnp.bfloat16)
        grad_a(g).start()

    def attend(g, b):
        cols = pl.ds(pl.multiple_of(g * (groups * HD), groups * HD), groups * HD)
        picks = [index_ref[b, s] for s in range(slots)]
        keys = jnp.concatenate([current[0, w] for w in picks], axis=0)
        values = jnp.concatenate([current[1, w] for w in picks], axis=0)
        keys_t = jnp.concatenate([turned[0, w] for w in picks], axis=1)
        values_t = jnp.concatenate([turned[1, w] for w in picks], axis=1)
        query_all = query_ref[b, :, cols]
        grad_all = grad_ref[b, :, cols]
        mask = jnp.concatenate([bias[b], bias[b]], axis=1)
        dkeys = dvalues = None
        for pair in range(groups // 2):
            tiles = [2 * pair, 2 * pair + 1]
            query = jnp.concatenate([query_all[:, j * HD:(j + 1) * HD] for j in tiles], axis=0)
            grad = jnp.concatenate([grad_all[:, j * HD:(j + 1) * HD] for j in tiles], axis=0)
            nt = (((1,), (1,)), ((), ()))
            scores = lax.dot_general(keys, query, nt, preferred_element_type=jnp.float32)
            dprobs = lax.dot_general(values, grad, nt, preferred_element_type=jnp.float32)
            scores = scores * scale2 + mask
            top = jnp.max(scores, axis=0, keepdims=True)
            probs = jnp.exp2(scores - top)
            probs = probs * (1.0 / jnp.sum(probs, axis=0, keepdims=True))
            low = probs.astype(jnp.bfloat16)
            out_t = jnp.dot(values_t, low, preferred_element_type=jnp.float32).astype(jnp.bfloat16)
            delta = jnp.sum(
                out_t.astype(jnp.float32) * grad.T.astype(jnp.float32), axis=0, keepdims=True
            )
            dscores = (probs * (dprobs - delta)).astype(jnp.bfloat16)
            dquery_t = (
                jnp.dot(keys_t, dscores, preferred_element_type=jnp.float32) * scaling
            ).astype(jnp.bfloat16)
            for at, j in enumerate(tiles):
                spot = pl.ds(pl.multiple_of(g * (groups * HD) + j * HD, HD), HD)
                out_ref[b, :, spot] = out_t[:, at * BLOCK:(at + 1) * BLOCK].T
                dquery_ref[b, :, spot] = dquery_t[:, at * BLOCK:(at + 1) * BLOCK].T
            dkey = jnp.dot(dscores, query, preferred_element_type=jnp.float32)
            dvalue = jnp.dot(low, grad, preferred_element_type=jnp.float32)
            dkeys = dkey if dkeys is None else dkeys + dkey
            dvalues = dvalue if dvalues is None else dvalues + dvalue
        parts[0, pl.ds(b * slots, slots)] = (dkeys * scaling).reshape(slots, BLOCK, HD)
        parts[1, pl.ds(b * slots, slots)] = dvalues.reshape(slots, BLOCK, HD)

    def head(g, _):
        copy_b(g, here).wait_recv()
        for kind in range(2):
            for w in range((R_DEV + 1) * blocks):
                tile = window[g, kind, w]
                current[kind, w] = tile
                turned[kind, w] = tile.T

        def block(b, _):
            @pl.when(jnp.logical_and(b == blocks - 1, g < kv_heads - 1))
            def _():
                arrive(g + 1)

            @pl.when(jnp.logical_and(jnp.logical_and(b == 1, g > 0), odd))
            def _():
                forward_grad(g - 1)

            attend(g, b)
            return 0

        lax.fori_loop(0, blocks, block, 0)
        for kind in range(2):
            for w in range(2 * blocks):
                total = parts[kind, inverse_ref[0, w]]
                for b in range(1, blocks):
                    total = total + parts[kind, inverse_ref[b, w]]
                into, at = (send_a, w) if w < blocks else (send_b, w - blocks)
                into[g, kind, at] = total.astype(jnp.bfloat16)
        grad_b(g).start()

        @pl.when(even)
        def _():
            grad_a(g).start()

        for kind in range(2):
            for j in range(blocks):
                total = parts[kind, j * slots]
                for b in range(j + 1, blocks):
                    total = total + parts[kind, inverse_ref[b, 2 * blocks + j]]
                own[g, kind, j] = total
        return 0

    arrive(0)
    lax.fori_loop(0, kv_heads, head, 0)

    @pl.when(odd)
    def _():
        forward_grad(kv_heads - 1)

    for g in range(kv_heads):
        @pl.when(even)
        def _():
            grad_b(g).wait_recv()
            own[g] = own[g] + take_b[g].astype(jnp.float32)

        grad_a(g).wait_recv()
        cols = pl.ds(g * HD, HD)
        for kind, ref in enumerate((dkey_ref, dvalue_ref)):
            ref[:, :, cols] = (own[g, kind] + take_a[g, kind].astype(jnp.float32)).astype(
                jnp.bfloat16
            )
    for g in range(kv_heads):
        copy_a(g).wait_send()

        @pl.when(even)
        def _():
            copy_b(g, here).wait_send()

        @pl.when(odd)
        def _():
            copy_b(g, far).wait_send()

        grad_a(g).wait_send()
        grad_b(g).wait_send()


def per_device(n, queries, keys, values, out_grad, doc_starts, block_lists):
    device = lax.axis_index("ctx")
    blocks, slots = block_lists.shape
    rows = queries.shape[0]
    kv_heads = keys.shape[1] // HD
    groups = queries.shape[1] // keys.shape[1]
    window_blocks = (R_DEV + 1) * blocks
    listed = block_lists >= 0
    at = block_lists - (device - R_DEV) * blocks
    index = jnp.where(listed, at, R_DEV * blocks)
    base = jnp.where(listed, block_lists * BLOCK, FAR)
    hit = (at[:, :, None] == jnp.arange(window_blocks)[None, None, :]) & listed[:, :, None]
    place = jnp.arange(blocks)[:, None, None] * slots + jnp.arange(slots)[None, :, None]
    inverse = jnp.min(jnp.where(hit, place, blocks * slots), axis=1).astype(jnp.int32)
    wide, slim = queries.shape[1], keys.shape[1]

    def shaped(array):
        return array.reshape(blocks, BLOCK, array.shape[1])

    smem = pl.BlockSpec(memory_space=pltpu.SMEM)
    vmem = pl.BlockSpec(memory_space=pltpu.VMEM)
    hbm = pl.BlockSpec(memory_space=pl.ANY)
    bf16, f32 = jnp.bfloat16, jnp.float32
    chunk = (kv_heads, 2, blocks, BLOCK, HD)
    dma = pltpu.SemaphoreType.DMA
    results = pl.pallas_call(
        functools.partial(kernel, n, blocks, slots, kv_heads, groups),
        out_shape=(
            jax.ShapeDtypeStruct((blocks, BLOCK, wide), bf16),
            jax.ShapeDtypeStruct((blocks, BLOCK, wide), bf16),
            jax.ShapeDtypeStruct((blocks, BLOCK, slim), bf16),
            jax.ShapeDtypeStruct((blocks, BLOCK, slim), bf16),
        ),
        in_specs=[smem] * 4 + [hbm] * 2 + [vmem] * 2,
        out_specs=[vmem] * 4,
        scratch_shapes=[
            pltpu.VMEM((kv_heads, 2, window_blocks, BLOCK, HD), bf16),
            pltpu.VMEM((2, window_blocks, BLOCK, HD), bf16),
            pltpu.VMEM((2, window_blocks, BLOCK, HD), bf16),
            pltpu.VMEM((blocks, slots * BLOCK, BLOCK), f32),
            pltpu.VMEM((2, blocks * slots + 1, BLOCK, HD), f32),
            pltpu.VMEM(chunk, f32),
            pltpu.VMEM(chunk, bf16),
            pltpu.VMEM(chunk, bf16),
            pltpu.VMEM(chunk, bf16),
            pltpu.VMEM(chunk, bf16),
            dma((kv_heads, 2)),
        ] + [dma((kv_heads,))] * 8,
        compiler_params=pltpu.CompilerParams(
            collective_id=0, has_side_effects=True, vmem_limit_bytes=56 * 1024 * 1024
        ),
        cost_estimate=pl.CostEstimate(
            flops=12 * rows * wide * slots * BLOCK,
            bytes_accessed=8 * rows * (wide + slim),
            transcendentals=rows * (wide // HD) * slots * BLOCK,
        ),
    )(
        index.astype(jnp.int32), base.astype(jnp.int32), inverse, doc_starts,
        shaped(keys), shaped(values), shaped(queries), shaped(out_grad),
    )
    return tuple(result.reshape(rows, result.shape[2]) for result in results)


def solution(mesh):
    both = P(("grp", "ctx"), None)
    return jax.shard_map(
        functools.partial(per_device, mesh.shape["ctx"]),
        mesh=mesh,
        in_specs=(both, both, both, both, P("grp"), both),
        out_specs=(both, both, both, both),
        check_vma=False,
    )
```

```python
import functools

import jax
import jax.numpy as jnp
from jax import lax
from jax.experimental import pallas as pl
from jax.experimental.pallas import tpu as pltpu
from jax.sharding import PartitionSpec as P

HD = 128
BLOCK = 128
R_DEV = 2
MESH = pl.DeviceIdType.MESH
FAR = 1 << 30


def kernel(
    n, blocks, slots, kv_heads, groups,
    lists_ref, starts_ref, key_hbm, value_hbm, query_hbm, grad_hbm,
    out_hbm, dquery_hbm, dkey_ref, dvalue_ref,
    window, current, turned, bias, parts, own, send_a, send_b, take_a, take_b,
    query_buf, grad_buf, out_buf, dquery_buf, inverse,
    local_sem, load_sem, store_sem,
    a_send, a_recv, b_send, b_recv, ga_send, ga_recv, gb_send, gb_recv,
):
    me = lax.axis_index("ctx")
    odd = lax.rem(me, 2) == 1
    even = jnp.logical_not(odd)
    partner = me + 1 - 2 * lax.rem(me, 2)
    ahead = lax.rem(me + 2, n)
    behind = lax.rem(me + n - 2, n)
    here = pl.ds(2 * blocks, blocks)
    near = pl.ds(blocks, blocks)
    far = pl.ds(0, blocks)
    wide = groups * HD
    scaling = HD ** (-0.5)
    scale2 = scaling * 1.4426950408889634
    window_base = (me - R_DEV) * blocks

    def local_copies(g):
        cols = pl.ds(pl.multiple_of(g * HD, HD), HD)
        return [
            pltpu.make_async_copy(
                ref.at[:, :, cols], window.at[g, kind, here], local_sem.at[g, kind]
            )
            for kind, ref in enumerate((key_hbm, value_hbm))
        ]

    def loads(g):
        cols = pl.ds(pl.multiple_of(g * wide, wide), wide)
        return [
            pltpu.make_async_copy(ref.at[:, :, cols], buf.at[:, :, cols], load_sem.at[g, kind])
            for kind, (ref, buf) in enumerate(((query_hbm, query_buf), (grad_hbm, grad_buf)))
        ]

    def stores(g):
        cols = pl.ds(pl.multiple_of(g * wide, wide), wide)
        return [
            pltpu.make_async_copy(buf.at[:, :, cols], ref.at[:, :, cols], store_sem.at[g, kind])
            for kind, (ref, buf) in enumerate(((out_hbm, out_buf), (dquery_hbm, dquery_buf)))
        ]

    def remote(src, dst, send, recv, target):
        return pltpu.make_async_remote_copy(
            src_ref=src, dst_ref=dst, send_sem=send, recv_sem=recv,
            device_id={"ctx": target}, device_id_type=MESH,
        )

    def copy_a(g):
        return remote(
            window.at[g, :, here], window.at[g, :, far], a_send.at[g], a_recv.at[g], ahead
        )

    def copy_b(g, source):
        return remote(
            window.at[g, :, source], window.at[g, :, near], b_send.at[g], b_recv.at[g], partner
        )

    def grad_a(g):
        return remote(send_a.at[g], take_a.at[g], ga_send.at[g], ga_recv.at[g], behind)

    def grad_b(g):
        return remote(send_b.at[g], take_b.at[g], gb_send.at[g], gb_recv.at[g], partner)

    barrier = pltpu.get_barrier_semaphore()
    for other in (ahead, behind, partner):
        pl.semaphore_signal(barrier, inc=1, device_id={"ctx": other}, device_id_type=MESH)
    for g in range(kv_heads):
        for copy in local_copies(g):
            copy.start()
    for g in range(kv_heads):
        for copy in loads(g):
            copy.start()
    pl.semaphore_wait(barrier, 3)
    for g in range(kv_heads):
        for copy in local_copies(g):
            copy.wait()
        if g == 0:
            copy_a(g).start()

        @pl.when(even)
        def _():
            copy_b(g, here).start()

    parts[:, blocks * slots] = jnp.zeros((2, BLOCK, HD), jnp.float32)
    for b in range(blocks):
        for w in range((R_DEV + 1) * blocks):
            found = jnp.int32(blocks * slots)
            for s in range(slots):
                found = jnp.where(lists_ref[b, s] == window_base + w, b * slots + s, found)
            inverse[b, w] = jnp.where(window_base + w >= 0, found, blocks * slots)
    first = me * (blocks * BLOCK)
    lanes = lax.broadcasted_iota(jnp.int32, (1, BLOCK), 1)
    rows = lax.broadcasted_iota(jnp.int32, (BLOCK, BLOCK), 0)
    for b in range(blocks):
        pos = first + b * BLOCK + lanes
        low = jnp.zeros_like(pos)
        for d in range(starts_ref.shape[0]):
            start = starts_ref[d]
            low = jnp.maximum(low, jnp.where(start <= pos, start, 0))
        for s in range(slots):
            entry = lists_ref[b, s]
            at = jnp.where(entry >= 0, entry * BLOCK, FAR) + rows
            keep = jnp.logical_and(at <= pos, at >= low)
            bias[b, pl.ds(s * BLOCK, BLOCK), :] = jnp.where(keep, 0.0, -1e30).astype(jnp.bfloat16)
    copy_a(0).wait_send()
    copy_a(1).start()

    def arrive(g):
        copy_a(g).wait_recv()

        @pl.when(odd)
        def _():
            copy_b(g, far).start()

    def forward_grad(g):
        grad_b(g).wait_recv()
        send_a[g] = (
            send_a[g].astype(jnp.float32) + take_b[g].astype(jnp.float32)
        ).astype(jnp.bfloat16)
        grad_a(g).start()

    nt = (((1,), (1,)), ((), ()))
    square = lax.broadcasted_iota(jnp.int32, (BLOCK, BLOCK), 1) == rows
    one_hot = jnp.where(square, 1.0, 0.0).astype(jnp.bfloat16)
    one_hot = jnp.concatenate([one_hot, one_hot], axis=0)

    def attend(g, half):
        pairs = groups // 2
        chains = [(at, pair) for at in range(blocks // 2) for pair in range(pairs)]

        def place(at):
            return half * (blocks // 2) + at

        def picks(at):
            found = []
            for s in range(slots):
                entry = lists_ref[place(at), s]
                spot = jnp.where(entry >= 0, entry - window_base, R_DEV * blocks)
                found.append(jnp.clip(spot, 0, (R_DEV + 1) * blocks - 1))
            return found

        tiles = {}

        def score(chain):
            at, pair = chain
            b = place(at)
            if at not in tiles:
                found = picks(at)
                keys = jnp.concatenate([current[0, w] for w in found], axis=0)
                tiles[at] = (found, jnp.concatenate([keys, bias[b]], axis=1))
            spot = pl.ds(pl.multiple_of(g * wide + pair * 2 * HD, 2 * HD), 2 * HD)
            query_two = query_buf[b, :, spot]
            query = jnp.concatenate([query_two[:, :HD], query_two[:, HD:]], axis=0)
            deep = jnp.concatenate([query, one_hot], axis=1)
            return query, lax.dot_general(
                tiles[at][1], deep, nt, preferred_element_type=jnp.float32
            )

        sums = {}

        def rest(chain, query, scores):
            at, pair = chain
            b = place(at)
            found = tiles[at][0]
            spot = pl.ds(pl.multiple_of(g * wide + pair * 2 * HD, 2 * HD), 2 * HD)
            grad_two = grad_buf[b, :, spot]
            grad_t = jnp.concatenate([grad_two[:, :HD].T, grad_two[:, HD:].T], axis=1)
            values = jnp.concatenate([current[1, w] for w in found], axis=0)
            keys_t = jnp.concatenate([turned[0, w] for w in found], axis=1)
            values_t = jnp.concatenate([turned[1, w] for w in found], axis=1)
            top = jnp.max(scores, axis=0, keepdims=True) * scale2
            probs = jnp.exp2(scores * scale2 - top)
            inv = 1.0 / jnp.sum(probs, axis=0, keepdims=True)
            grad_t = (grad_t.astype(jnp.float32) * inv).astype(jnp.bfloat16)
            dprobs = jnp.dot(values, grad_t, preferred_element_type=jnp.float32)
            low = probs.astype(jnp.bfloat16)
            out_t = jnp.dot(values_t, low, preferred_element_type=jnp.float32)
            out_t = (out_t * inv).astype(jnp.bfloat16)
            delta = jnp.sum(
                out_t.astype(jnp.float32) * grad_t.astype(jnp.float32), axis=0, keepdims=True
            )
            dscores = (probs * (dprobs - delta)).astype(jnp.bfloat16)
            dvalue = lax.dot_general(low, grad_t, nt, preferred_element_type=jnp.float32)
            dquery_t = (
                jnp.dot(keys_t, dscores, preferred_element_type=jnp.float32) * scaling
            ).astype(jnp.bfloat16)
            dkey = jnp.dot(dscores, query, preferred_element_type=jnp.float32)
            out_buf[b, :, spot] = jnp.concatenate([out_t[:, :BLOCK].T, out_t[:, BLOCK:].T], axis=1)
            dquery_buf[b, :, spot] = jnp.concatenate(
                [dquery_t[:, :BLOCK].T, dquery_t[:, BLOCK:].T], axis=1
            )
            if pair == 0:
                sums[at] = (dkey, dvalue)
            else:
                sums[at] = (sums[at][0] + dkey, sums[at][1] + dvalue)
            if pair == pairs - 1:
                kept = pl.ds(b * slots, slots)
                parts[0, kept] = (sums[at][0] * scaling).reshape(slots, BLOCK, HD)
                parts[1, kept] = sums[at][1].reshape(slots, BLOCK, HD)

        ready = score(chains[0])
        for i, chain in enumerate(chains):
            now = ready
            if i + 1 < len(chains):
                ready = score(chains[i + 1])
            rest(chain, *now)

    def head(g, _):
        copy_b(g, here).wait_recv()
        for copy in loads(g):
            copy.wait()
        for kind in range(2):
            for w in range((R_DEV + 1) * blocks):
                tile = window[g, kind, w]
                current[kind, w] = tile
                turned[kind, w] = tile.T

        def block(half, _):
            @pl.when(half == 1)
            def _():
                @pl.when(g < kv_heads - 2)
                def _():
                    copy_a(g + 1).wait_send()
                    copy_a(g + 2).start()

                @pl.when(g < kv_heads - 1)
                def _():
                    arrive(g + 1)

                @pl.when(jnp.logical_and(g > 0, odd))
                def _():
                    forward_grad(g - 1)

            attend(g, half)
            return 0

        lax.fori_loop(0, 2, block, 0)
        for kind in range(2):
            for w in range(blocks, 2 * blocks):
                total = parts[kind, inverse[0, w]]
                for b in range(1, blocks):
                    total = total + parts[kind, inverse[b, w]]
                send_b[g, kind, w - blocks] = total.astype(jnp.bfloat16)
        grad_b(g).start()
        for kind in range(2):
            for w in range(blocks):
                total = parts[kind, inverse[0, w]]
                for b in range(1, blocks):
                    total = total + parts[kind, inverse[b, w]]
                send_a[g, kind, w] = total.astype(jnp.bfloat16)

        @pl.when(even)
        def _():
            grad_a(g).start()

        for copy in stores(g):
            copy.start()
        for kind in range(2):
            for j in range(blocks):
                total = parts[kind, j * slots]
                for b in range(j + 1, blocks):
                    total = total + parts[kind, inverse[b, 2 * blocks + j]]
                own[g, kind, j] = total
        return 0

    arrive(0)
    lax.fori_loop(0, kv_heads, head, 0)

    @pl.when(odd)
    def _():
        forward_grad(kv_heads - 1)

    for g in range(kv_heads):
        @pl.when(even)
        def _():
            grad_b(g).wait_recv()
            own[g] = own[g] + take_b[g].astype(jnp.float32)

        grad_a(g).wait_recv()
        cols = pl.ds(g * HD, HD)
        for kind, ref in enumerate((dkey_ref, dvalue_ref)):
            ref[:, :, cols] = (own[g, kind] + take_a[g, kind].astype(jnp.float32)).astype(
                jnp.bfloat16
            )
    copy_a(kv_heads - 1).wait_send()
    for g in range(kv_heads):
        @pl.when(even)
        def _():
            copy_b(g, here).wait_send()

        @pl.when(odd)
        def _():
            copy_b(g, far).wait_send()

        grad_a(g).wait_send()
        grad_b(g).wait_send()
        for copy in stores(g):
            copy.wait()


def per_device(n, queries, keys, values, out_grad, doc_starts, block_lists):
    blocks, slots = block_lists.shape
    rows = queries.shape[0]
    kv_heads = keys.shape[1] // HD
    groups = queries.shape[1] // keys.shape[1]
    window_blocks = (R_DEV + 1) * blocks
    wide, slim = queries.shape[1], keys.shape[1]

    def shaped(array):
        return array.reshape(blocks, BLOCK, array.shape[1])

    smem = pl.BlockSpec(memory_space=pltpu.SMEM)
    vmem = pl.BlockSpec(memory_space=pltpu.VMEM)
    hbm = pl.BlockSpec(memory_space=pl.ANY)
    bf16, f32 = jnp.bfloat16, jnp.float32
    chunk = (kv_heads, 2, blocks, BLOCK, HD)
    dma = pltpu.SemaphoreType.DMA
    results = pl.pallas_call(
        functools.partial(kernel, n, blocks, slots, kv_heads, groups),
        out_shape=(
            jax.ShapeDtypeStruct((blocks, BLOCK, wide), bf16),
            jax.ShapeDtypeStruct((blocks, BLOCK, wide), bf16),
            jax.ShapeDtypeStruct((blocks, BLOCK, slim), bf16),
            jax.ShapeDtypeStruct((blocks, BLOCK, slim), bf16),
        ),
        in_specs=[smem] * 2 + [hbm] * 4,
        out_specs=[hbm] * 2 + [vmem] * 2,
        scratch_shapes=[
            pltpu.VMEM((kv_heads, 2, window_blocks, BLOCK, HD), bf16),
            pltpu.VMEM((2, window_blocks, BLOCK, HD), bf16),
            pltpu.VMEM((2, window_blocks, BLOCK, HD), bf16),
            pltpu.VMEM((blocks, slots * BLOCK, BLOCK), bf16),
            pltpu.VMEM((2, blocks * slots + 1, BLOCK, HD), f32),
            pltpu.VMEM(chunk, f32),
            pltpu.VMEM(chunk, bf16),
            pltpu.VMEM(chunk, bf16),
            pltpu.VMEM(chunk, bf16),
            pltpu.VMEM(chunk, bf16),
        ] + [pltpu.VMEM((blocks, BLOCK, wide), bf16)] * 4 + [
            pltpu.SMEM((blocks, window_blocks), jnp.int32),
        ] + [dma((kv_heads, 2))] * 3 + [dma((kv_heads,))] * 8,
        compiler_params=pltpu.CompilerParams(
            collective_id=0, has_side_effects=True, vmem_limit_bytes=56 * 1024 * 1024
        ),
        cost_estimate=pl.CostEstimate(
            flops=12 * rows * wide * slots * BLOCK,
            bytes_accessed=8 * rows * (wide + slim),
            transcendentals=rows * (wide // HD) * slots * BLOCK,
        ),
    )(
        block_lists, doc_starts, shaped(keys), shaped(values), shaped(queries), shaped(out_grad),
    )
    return tuple(result.reshape(rows, result.shape[2]) for result in results)


def solution(mesh):
    both = P(("grp", "ctx"), None)
    return jax.shard_map(
        functools.partial(per_device, mesh.shape["ctx"]),
        mesh=mesh,
        in_specs=(both, both, both, both, P("grp"), both),
        out_specs=(both, both, both, both),
        check_vma=False,
    )
```

```python
import functools

import jax
import jax.numpy as jnp
from jax import lax
from jax.experimental import pallas as pl
from jax.experimental.pallas import tpu as pltpu
from jax.sharding import PartitionSpec as P

HD = 128
BLOCK = 128
R_DEV = 2
MESH = pl.DeviceIdType.MESH
FAR = 1 << 30


def kernel(
    n, blocks, slots, kv_heads, groups,
    lists_ref, starts_ref, key_hbm, value_hbm, query_hbm, grad_hbm,
    out_hbm, dquery_hbm, dkey_ref, dvalue_ref,
    window, current, turned, bias, parts, own, send_a, send_b, take_a, take_b,
    query_buf, grad_buf, out_buf, dquery_buf, inverse,
    local_sem, load_sem, store_sem,
    a_send, a_recv, b_send, b_recv, ga_send, ga_recv, gb_send, gb_recv,
):
    me = lax.axis_index("ctx")
    odd = lax.rem(me, 2) == 1
    even = jnp.logical_not(odd)
    partner = me + 1 - 2 * lax.rem(me, 2)
    ahead = lax.rem(me + 2, n)
    behind = lax.rem(me + n - 2, n)
    here = pl.ds(2 * blocks, blocks)
    near = pl.ds(blocks, blocks)
    far = pl.ds(0, blocks)
    wide = groups * HD
    scaling = HD ** (-0.5)
    scale2 = scaling * 1.4426950408889634
    window_base = (me - R_DEV) * blocks

    def local_copies(g):
        cols = pl.ds(pl.multiple_of(g * HD, HD), HD)
        return [
            pltpu.make_async_copy(
                ref.at[:, :, cols], window.at[g, kind, here], local_sem.at[g, kind]
            )
            for kind, ref in enumerate((key_hbm, value_hbm))
        ]

    def loads(g):
        cols = pl.ds(pl.multiple_of(g * wide, wide), wide)
        return [
            pltpu.make_async_copy(ref.at[:, :, cols], buf.at[:, :, cols], load_sem.at[g, kind])
            for kind, (ref, buf) in enumerate(((query_hbm, query_buf), (grad_hbm, grad_buf)))
        ]

    def stores(g):
        cols = pl.ds(pl.multiple_of(g * wide, wide), wide)
        return [
            pltpu.make_async_copy(buf.at[:, :, cols], ref.at[:, :, cols], store_sem.at[g, kind])
            for kind, (ref, buf) in enumerate(((out_hbm, out_buf), (dquery_hbm, dquery_buf)))
        ]

    def remote(src, dst, send, recv, target):
        return pltpu.make_async_remote_copy(
            src_ref=src, dst_ref=dst, send_sem=send, recv_sem=recv,
            device_id={"ctx": target}, device_id_type=MESH,
        )

    def copy_a(g):
        return remote(
            window.at[g, :, here], window.at[g, :, far], a_send.at[g], a_recv.at[g], ahead
        )

    def copy_b(g, source):
        return remote(
            window.at[g, :, source], window.at[g, :, near], b_send.at[g], b_recv.at[g], partner
        )

    def grad_a(g):
        return remote(send_a.at[g], take_a.at[g], ga_send.at[g], ga_recv.at[g], behind)

    def grad_b(g):
        return remote(send_b.at[g], take_b.at[g], gb_send.at[g], gb_recv.at[g], partner)

    barrier = pltpu.get_barrier_semaphore()
    for other in (ahead, behind, partner):
        pl.semaphore_signal(barrier, inc=1, device_id={"ctx": other}, device_id_type=MESH)
    for g in range(kv_heads):
        for copy in local_copies(g):
            copy.start()
    for g in range(kv_heads):
        for copy in loads(g):
            copy.start()
    pl.semaphore_wait(barrier, 3)
    for g in range(kv_heads):
        for copy in local_copies(g):
            copy.wait()
        if g == 0:
            copy_a(g).start()

        @pl.when(even)
        def _():
            copy_b(g, here).start()

    parts[:, blocks * slots] = jnp.zeros((2, BLOCK, HD), jnp.float32)
    for b in range(blocks):
        for w in range((R_DEV + 1) * blocks):
            found = jnp.int32(blocks * slots)
            for s in range(slots):
                found = jnp.where(lists_ref[b, s] == window_base + w, b * slots + s, found)
            inverse[b, w] = jnp.where(window_base + w >= 0, found, blocks * slots)
    first = me * (blocks * BLOCK)
    lanes = lax.broadcasted_iota(jnp.int32, (1, BLOCK), 1)
    rows = lax.broadcasted_iota(jnp.int32, (BLOCK, BLOCK), 0)
    for b in range(blocks):
        pos = first + b * BLOCK + lanes
        low = jnp.zeros_like(pos)
        for d in range(starts_ref.shape[0]):
            start = starts_ref[d]
            low = jnp.maximum(low, jnp.where(start <= pos, start, 0))
        for s in range(slots):
            entry = lists_ref[b, s]
            at = jnp.where(entry >= 0, entry * BLOCK, FAR) + rows
            keep = jnp.logical_and(at <= pos, at >= low)
            bias[b, pl.ds(s * BLOCK, BLOCK), :] = jnp.where(keep, 0.0, -1e30)
    copy_a(0).wait_send()
    copy_a(1).start()

    def arrive(g):
        copy_a(g).wait_recv()

        @pl.when(odd)
        def _():
            copy_b(g, far).start()

    def forward_grad(g):
        grad_b(g).wait_recv()
        send_a[g] = (
            send_a[g].astype(jnp.float32) + take_b[g].astype(jnp.float32)
        ).astype(jnp.bfloat16)
        grad_a(g).start()

    def attend(g, b):
        cols = pl.ds(pl.multiple_of(g * (groups * HD), groups * HD), groups * HD)
        picks = []
        for s in range(slots):
            entry = lists_ref[b, s]
            spot = jnp.where(entry >= 0, entry - window_base, R_DEV * blocks)
            picks.append(jnp.clip(spot, 0, (R_DEV + 1) * blocks - 1))
        keys = jnp.concatenate([current[0, w] for w in picks], axis=0)
        values = jnp.concatenate([current[1, w] for w in picks], axis=0)
        keys_t = jnp.concatenate([turned[0, w] for w in picks], axis=1)
        values_t = jnp.concatenate([turned[1, w] for w in picks], axis=1)
        query_all = query_buf[b, :, cols]
        grad_all = grad_buf[b, :, cols]
        mask = jnp.concatenate([bias[b], bias[b]], axis=1)
        dkeys = dvalues = None
        for pair in range(groups // 2):
            tiles = [2 * pair, 2 * pair + 1]
            query = jnp.concatenate([query_all[:, j * HD:(j + 1) * HD] for j in tiles], axis=0)
            grad = jnp.concatenate([grad_all[:, j * HD:(j + 1) * HD] for j in tiles], axis=0)
            nt = (((1,), (1,)), ((), ()))
            scores = lax.dot_general(keys, query, nt, preferred_element_type=jnp.float32)
            dprobs = lax.dot_general(values, grad, nt, preferred_element_type=jnp.float32)
            scores = scores * scale2 + mask
            top = jnp.max(scores, axis=0, keepdims=True)
            probs = jnp.exp2(scores - top)
            probs = probs * (1.0 / jnp.sum(probs, axis=0, keepdims=True))
            low = probs.astype(jnp.bfloat16)
            out_t = jnp.dot(values_t, low, preferred_element_type=jnp.float32).astype(jnp.bfloat16)
            delta = jnp.sum(
                out_t.astype(jnp.float32) * grad.T.astype(jnp.float32), axis=0, keepdims=True
            )
            dscores = (probs * (dprobs - delta)).astype(jnp.bfloat16)
            dquery_t = (
                jnp.dot(keys_t, dscores, preferred_element_type=jnp.float32) * scaling
            ).astype(jnp.bfloat16)
            for at, j in enumerate(tiles):
                spot = pl.ds(pl.multiple_of(g * (groups * HD) + j * HD, HD), HD)
                out_buf[b, :, spot] = out_t[:, at * BLOCK:(at + 1) * BLOCK].T
                dquery_buf[b, :, spot] = dquery_t[:, at * BLOCK:(at + 1) * BLOCK].T
            dkey = jnp.dot(dscores, query, preferred_element_type=jnp.float32)
            dvalue = jnp.dot(low, grad, preferred_element_type=jnp.float32)
            dkeys = dkey if dkeys is None else dkeys + dkey
            dvalues = dvalue if dvalues is None else dvalues + dvalue
        parts[0, pl.ds(b * slots, slots)] = (dkeys * scaling).reshape(slots, BLOCK, HD)
        parts[1, pl.ds(b * slots, slots)] = dvalues.reshape(slots, BLOCK, HD)

    def head(g, _):
        copy_b(g, here).wait_recv()
        for copy in loads(g):
            copy.wait()
        for kind in range(2):
            for w in range((R_DEV + 1) * blocks):
                tile = window[g, kind, w]
                current[kind, w] = tile
                turned[kind, w] = tile.T

        def block(b, _):
            @pl.when(b == blocks // 2)
            def _():
                @pl.when(g < kv_heads - 2)
                def _():
                    copy_a(g + 1).wait_send()
                    copy_a(g + 2).start()

                @pl.when(g < kv_heads - 1)
                def _():
                    arrive(g + 1)

                @pl.when(jnp.logical_and(g > 0, odd))
                def _():
                    forward_grad(g - 1)

            attend(g, b)
            return 0

        lax.fori_loop(0, blocks, block, 0)
        for kind in range(2):
            for w in range(blocks, 2 * blocks):
                total = parts[kind, inverse[0, w]]
                for b in range(1, blocks):
                    total = total + parts[kind, inverse[b, w]]
                send_b[g, kind, w - blocks] = total.astype(jnp.bfloat16)
        grad_b(g).start()
        for kind in range(2):
            for w in range(blocks):
                total = parts[kind, inverse[0, w]]
                for b in range(1, blocks):
                    total = total + parts[kind, inverse[b, w]]
                send_a[g, kind, w] = total.astype(jnp.bfloat16)

        @pl.when(even)
        def _():
            grad_a(g).start()

        for copy in stores(g):
            copy.start()
        for kind in range(2):
            for j in range(blocks):
                total = parts[kind, j * slots]
                for b in range(j + 1, blocks):
                    total = total + parts[kind, inverse[b, 2 * blocks + j]]
                own[g, kind, j] = total
        return 0

    arrive(0)
    lax.fori_loop(0, kv_heads, head, 0)

    @pl.when(odd)
    def _():
        forward_grad(kv_heads - 1)

    for g in range(kv_heads):
        @pl.when(even)
        def _():
            grad_b(g).wait_recv()
            own[g] = own[g] + take_b[g].astype(jnp.float32)

        grad_a(g).wait_recv()
        cols = pl.ds(g * HD, HD)
        for kind, ref in enumerate((dkey_ref, dvalue_ref)):
            ref[:, :, cols] = (own[g, kind] + take_a[g, kind].astype(jnp.float32)).astype(
                jnp.bfloat16
            )
    copy_a(kv_heads - 1).wait_send()
    for g in range(kv_heads):
        @pl.when(even)
        def _():
            copy_b(g, here).wait_send()

        @pl.when(odd)
        def _():
            copy_b(g, far).wait_send()

        grad_a(g).wait_send()
        grad_b(g).wait_send()
        for copy in stores(g):
            copy.wait()


def per_device(n, queries, keys, values, out_grad, doc_starts, block_lists):
    blocks, slots = block_lists.shape
    rows = queries.shape[0]
    kv_heads = keys.shape[1] // HD
    groups = queries.shape[1] // keys.shape[1]
    window_blocks = (R_DEV + 1) * blocks
    wide, slim = queries.shape[1], keys.shape[1]

    def shaped(array):
        return array.reshape(blocks, BLOCK, array.shape[1])

    smem = pl.BlockSpec(memory_space=pltpu.SMEM)
    vmem = pl.BlockSpec(memory_space=pltpu.VMEM)
    hbm = pl.BlockSpec(memory_space=pl.ANY)
    bf16, f32 = jnp.bfloat16, jnp.float32
    chunk = (kv_heads, 2, blocks, BLOCK, HD)
    dma = pltpu.SemaphoreType.DMA
    results = pl.pallas_call(
        functools.partial(kernel, n, blocks, slots, kv_heads, groups),
        out_shape=(
            jax.ShapeDtypeStruct((blocks, BLOCK, wide), bf16),
            jax.ShapeDtypeStruct((blocks, BLOCK, wide), bf16),
            jax.ShapeDtypeStruct((blocks, BLOCK, slim), bf16),
            jax.ShapeDtypeStruct((blocks, BLOCK, slim), bf16),
        ),
        in_specs=[smem] * 2 + [hbm] * 4,
        out_specs=[hbm] * 2 + [vmem] * 2,
        scratch_shapes=[
            pltpu.VMEM((kv_heads, 2, window_blocks, BLOCK, HD), bf16),
            pltpu.VMEM((2, window_blocks, BLOCK, HD), bf16),
            pltpu.VMEM((2, window_blocks, BLOCK, HD), bf16),
            pltpu.VMEM((blocks, slots * BLOCK, BLOCK), f32),
            pltpu.VMEM((2, blocks * slots + 1, BLOCK, HD), f32),
            pltpu.VMEM(chunk, f32),
            pltpu.VMEM(chunk, bf16),
            pltpu.VMEM(chunk, bf16),
            pltpu.VMEM(chunk, bf16),
            pltpu.VMEM(chunk, bf16),
        ] + [pltpu.VMEM((blocks, BLOCK, wide), bf16)] * 4 + [
            pltpu.SMEM((blocks, window_blocks), jnp.int32),
        ] + [dma((kv_heads, 2))] * 3 + [dma((kv_heads,))] * 8,
        compiler_params=pltpu.CompilerParams(
            collective_id=0, has_side_effects=True, vmem_limit_bytes=56 * 1024 * 1024
        ),
        cost_estimate=pl.CostEstimate(
            flops=12 * rows * wide * slots * BLOCK,
            bytes_accessed=8 * rows * (wide + slim),
            transcendentals=rows * (wide // HD) * slots * BLOCK,
        ),
    )(
        block_lists, doc_starts, shaped(keys), shaped(values), shaped(queries), shaped(out_grad),
    )
    return tuple(result.reshape(rows, result.shape[2]) for result in results)


def solution(mesh):
    both = P(("grp", "ctx"), None)
    return jax.shard_map(
        functools.partial(per_device, mesh.shape["ctx"]),
        mesh=mesh,
        in_specs=(both, both, both, both, P("grp"), both),
        out_specs=(both, both, both, both),
        check_vma=False,
    )
```

```python
import functools

import jax
import jax.numpy as jnp
from jax import lax
from jax.experimental import pallas as pl
from jax.experimental.pallas import tpu as pltpu
from jax.sharding import PartitionSpec as P

HD = 128
BLOCK = 128
R_DEV = 2
MESH = pl.DeviceIdType.MESH
FAR = 1 << 30


def kernel(
    n, blocks, slots, kv_heads, groups,
    lists_ref, starts_ref, key_hbm, value_hbm, query_hbm, grad_hbm,
    out_hbm, dquery_hbm, dkey_ref, dvalue_ref,
    window, current, turned, bias, parts, own, send_a, send_b, take_a, take_b,
    query_buf, grad_buf, out_buf, dquery_buf, inverse,
    local_sem, load_sem, store_sem,
    a_send, a_recv, b_send, b_recv, ga_send, ga_recv, gb_send, gb_recv,
):
    me = lax.axis_index("ctx")
    odd = lax.rem(me, 2) == 1
    even = jnp.logical_not(odd)
    partner = me + 1 - 2 * lax.rem(me, 2)
    ahead = lax.rem(me + 2, n)
    behind = lax.rem(me + n - 2, n)
    here = pl.ds(2 * blocks, blocks)
    near = pl.ds(blocks, blocks)
    far = pl.ds(0, blocks)
    wide = groups * HD
    scaling = HD ** (-0.5)
    scale2 = scaling * 1.4426950408889634
    window_base = (me - R_DEV) * blocks

    def local_copies(g):
        cols = pl.ds(pl.multiple_of(g * HD, HD), HD)
        return [
            pltpu.make_async_copy(
                ref.at[:, :, cols], window.at[g, kind, here], local_sem.at[g, kind]
            )
            for kind, ref in enumerate((key_hbm, value_hbm))
        ]

    def loads(g):
        cols = pl.ds(pl.multiple_of(g * wide, wide), wide)
        return [
            pltpu.make_async_copy(ref.at[:, :, cols], buf.at[:, :, cols], load_sem.at[g, kind])
            for kind, (ref, buf) in enumerate(((query_hbm, query_buf), (grad_hbm, grad_buf)))
        ]

    def stores(g):
        cols = pl.ds(pl.multiple_of(g * wide, wide), wide)
        return [
            pltpu.make_async_copy(buf.at[:, :, cols], ref.at[:, :, cols], store_sem.at[g, kind])
            for kind, (ref, buf) in enumerate(((out_hbm, out_buf), (dquery_hbm, dquery_buf)))
        ]

    def remote(src, dst, send, recv, target):
        return pltpu.make_async_remote_copy(
            src_ref=src, dst_ref=dst, send_sem=send, recv_sem=recv,
            device_id={"ctx": target}, device_id_type=MESH,
        )

    def copy_a(g):
        return remote(
            window.at[g, :, here], window.at[g, :, far], a_send.at[g], a_recv.at[g], ahead
        )

    def copy_b(g, source):
        return remote(
            window.at[g, :, source], window.at[g, :, near], b_send.at[g], b_recv.at[g], partner
        )

    def grad_a(g):
        return remote(send_a.at[g], take_a.at[g], ga_send.at[g], ga_recv.at[g], behind)

    def grad_b(g):
        return remote(send_b.at[g], take_b.at[g], gb_send.at[g], gb_recv.at[g], partner)

    barrier = pltpu.get_barrier_semaphore()
    for other in (ahead, behind, partner):
        pl.semaphore_signal(barrier, inc=1, device_id={"ctx": other}, device_id_type=MESH)
    for g in range(kv_heads):
        for copy in local_copies(g):
            copy.start()
    for g in range(kv_heads):
        for copy in loads(g):
            copy.start()
    pl.semaphore_wait(barrier, 3)
    for g in range(kv_heads):
        for copy in local_copies(g):
            copy.wait()
        if g == 0:
            copy_a(g).start()

        @pl.when(even)
        def _():
            copy_b(g, here).start()

    parts[:, blocks * slots] = jnp.zeros((2, BLOCK, HD), jnp.float32)
    for b in range(blocks):
        for w in range((R_DEV + 1) * blocks):
            found = jnp.int32(blocks * slots)
            for s in range(slots):
                found = jnp.where(lists_ref[b, s] == window_base + w, b * slots + s, found)
            inverse[b, w] = jnp.where(window_base + w >= 0, found, blocks * slots)
    first = me * (blocks * BLOCK)
    lanes = lax.broadcasted_iota(jnp.int32, (1, BLOCK), 1)
    rows = lax.broadcasted_iota(jnp.int32, (BLOCK, BLOCK), 0)
    for b in range(blocks):
        pos = first + b * BLOCK + lanes
        low = jnp.zeros_like(pos)
        for d in range(starts_ref.shape[0]):
            start = starts_ref[d]
            low = jnp.maximum(low, jnp.where(start <= pos, start, 0))
        for s in range(slots):
            entry = lists_ref[b, s]
            at = jnp.where(entry >= 0, entry * BLOCK, FAR) + rows
            keep = jnp.logical_and(at <= pos, at >= low)
            bias[b, pl.ds(s * BLOCK, BLOCK), :] = jnp.where(keep, 0.0, -1e30)
    copy_a(0).wait_send()
    copy_a(1).start()

    def arrive(g):
        copy_a(g).wait_recv()

        @pl.when(odd)
        def _():
            copy_b(g, far).start()

    def forward_grad(g):
        grad_b(g).wait_recv()
        send_a[g] = (
            send_a[g].astype(jnp.float32) + take_b[g].astype(jnp.float32)
        ).astype(jnp.bfloat16)
        grad_a(g).start()

    def attend(g, b):
        cols = pl.ds(pl.multiple_of(g * (groups * HD), groups * HD), groups * HD)
        picks = []
        for s in range(slots):
            entry = lists_ref[b, s]
            spot = jnp.where(entry >= 0, entry - window_base, R_DEV * blocks)
            picks.append(jnp.clip(spot, 0, (R_DEV + 1) * blocks - 1))
        keys = jnp.concatenate([current[0, w] for w in picks], axis=0)
        values = jnp.concatenate([current[1, w] for w in picks], axis=0)
        keys_t = jnp.concatenate([turned[0, w] for w in picks], axis=1)
        values_t = jnp.concatenate([turned[1, w] for w in picks], axis=1)
        query_all = query_buf[b, :, cols]
        grad_all = grad_buf[b, :, cols]
        mask = jnp.concatenate([bias[b]] * groups, axis=1)
        query = jnp.concatenate(
            [query_all[:, j * HD:(j + 1) * HD] for j in range(groups)], axis=0
        )
        grad = jnp.concatenate([grad_all[:, j * HD:(j + 1) * HD] for j in range(groups)], axis=0)
        grad_t = jnp.concatenate(
            [grad_all[:, j * HD:(j + 1) * HD].T for j in range(groups)], axis=1
        )
        nt = (((1,), (1,)), ((), ()))
        scores = lax.dot_general(keys, query, nt, preferred_element_type=jnp.float32)
        dprobs = jnp.dot(values, grad_t, preferred_element_type=jnp.float32)
        scores = scores * scale2 + mask
        top = jnp.max(scores, axis=0, keepdims=True)
        probs = jnp.exp2(scores - top)
        probs = probs * (1.0 / jnp.sum(probs, axis=0, keepdims=True))
        low = probs.astype(jnp.bfloat16)
        out_t = jnp.dot(values_t, low, preferred_element_type=jnp.float32).astype(jnp.bfloat16)
        delta = jnp.sum(
            out_t.astype(jnp.float32) * grad_t.astype(jnp.float32), axis=0, keepdims=True
        )
        dscores = (probs * (dprobs - delta)).astype(jnp.bfloat16)
        dvalues = jnp.dot(low, grad, preferred_element_type=jnp.float32)
        dquery_t = (
            jnp.dot(keys_t, dscores, preferred_element_type=jnp.float32) * scaling
        ).astype(jnp.bfloat16)
        dkeys = jnp.dot(dscores, query, preferred_element_type=jnp.float32)
        for j in range(groups):
            spot = pl.ds(pl.multiple_of(g * wide + j * HD, HD), HD)
            out_buf[b, :, spot] = out_t[:, j * BLOCK:(j + 1) * BLOCK].T
            dquery_buf[b, :, spot] = dquery_t[:, j * BLOCK:(j + 1) * BLOCK].T
        parts[0, pl.ds(b * slots, slots)] = (dkeys * scaling).reshape(slots, BLOCK, HD)
        parts[1, pl.ds(b * slots, slots)] = dvalues.reshape(slots, BLOCK, HD)

    def head(g, _):
        copy_b(g, here).wait_recv()
        for copy in loads(g):
            copy.wait()
        for kind in range(2):
            for w in range((R_DEV + 1) * blocks):
                tile = window[g, kind, w]
                current[kind, w] = tile
                turned[kind, w] = tile.T

        def block(b, _):
            @pl.when(jnp.logical_and(b == 1, g < kv_heads - 2))
            def _():
                copy_a(g + 1).wait_send()
                copy_a(g + 2).start()

            @pl.when(jnp.logical_and(b == 1, jnp.logical_and(g > 0, odd)))
            def _():
                forward_grad(g - 1)

            @pl.when(jnp.logical_and(b == blocks - 1, g < kv_heads - 1))
            def _():
                arrive(g + 1)

            attend(g, b)
            return 0

        lax.fori_loop(0, blocks, block, 0)
        for kind in range(2):
            for w in range(blocks, 2 * blocks):
                total = parts[kind, inverse[0, w]]
                for b in range(1, blocks):
                    total = total + parts[kind, inverse[b, w]]
                send_b[g, kind, w - blocks] = total.astype(jnp.bfloat16)
        grad_b(g).start()
        for kind in range(2):
            for w in range(blocks):
                total = parts[kind, inverse[0, w]]
                for b in range(1, blocks):
                    total = total + parts[kind, inverse[b, w]]
                send_a[g, kind, w] = total.astype(jnp.bfloat16)

        @pl.when(even)
        def _():
            grad_a(g).start()

        for copy in stores(g):
            copy.start()
        for kind in range(2):
            for j in range(blocks):
                total = parts[kind, j * slots]
                for b in range(j + 1, blocks):
                    total = total + parts[kind, inverse[b, 2 * blocks + j]]
                own[g, kind, j] = total
        return 0

    arrive(0)
    lax.fori_loop(0, kv_heads, head, 0)

    @pl.when(odd)
    def _():
        forward_grad(kv_heads - 1)

    for g in range(kv_heads):
        @pl.when(even)
        def _():
            grad_b(g).wait_recv()
            own[g] = own[g] + take_b[g].astype(jnp.float32)

        grad_a(g).wait_recv()
        cols = pl.ds(g * HD, HD)
        for kind, ref in enumerate((dkey_ref, dvalue_ref)):
            ref[:, :, cols] = (own[g, kind] + take_a[g, kind].astype(jnp.float32)).astype(
                jnp.bfloat16
            )
    copy_a(kv_heads - 1).wait_send()
    for g in range(kv_heads):
        @pl.when(even)
        def _():
            copy_b(g, here).wait_send()

        @pl.when(odd)
        def _():
            copy_b(g, far).wait_send()

        grad_a(g).wait_send()
        grad_b(g).wait_send()
        for copy in stores(g):
            copy.wait()


def copy_kernel(*refs):
    sems = refs[8]
    copies = [
        pltpu.make_async_copy(refs[i].at[b], refs[4 + i].at[b], sems.at[i, b])
        for i in range(4)
        for b in range(refs[i].shape[0])
    ]
    for copy in copies:
        copy.start()
    for copy in copies:
        copy.wait()


def per_device(n, queries, keys, values, out_grad, doc_starts, block_lists):
    blocks, slots = block_lists.shape
    rows = queries.shape[0]
    kv_heads = keys.shape[1] // HD
    groups = queries.shape[1] // keys.shape[1]
    window_blocks = (R_DEV + 1) * blocks
    wide, slim = queries.shape[1], keys.shape[1]

    def shaped(array):
        return array.reshape(blocks, BLOCK, array.shape[1])

    smem = pl.BlockSpec(memory_space=pltpu.SMEM)
    vmem = pl.BlockSpec(memory_space=pltpu.VMEM)
    hbm = pl.BlockSpec(memory_space=pl.ANY)
    bf16, f32 = jnp.bfloat16, jnp.float32
    chunk = (kv_heads, 2, blocks, BLOCK, HD)
    dma = pltpu.SemaphoreType.DMA
    results = pl.pallas_call(
        functools.partial(kernel, n, blocks, slots, kv_heads, groups),
        out_shape=(
            jax.ShapeDtypeStruct((blocks, BLOCK, wide), bf16),
            jax.ShapeDtypeStruct((blocks, BLOCK, wide), bf16),
            jax.ShapeDtypeStruct((blocks, BLOCK, slim), bf16),
            jax.ShapeDtypeStruct((blocks, BLOCK, slim), bf16),
        ),
        in_specs=[smem] * 2 + [hbm] * 4,
        out_specs=[hbm] * 2 + [vmem] * 2,
        scratch_shapes=[
            pltpu.VMEM((kv_heads, 2, window_blocks, BLOCK, HD), bf16),
            pltpu.VMEM((2, window_blocks, BLOCK, HD), bf16),
            pltpu.VMEM((2, window_blocks, BLOCK, HD), bf16),
            pltpu.VMEM((blocks, slots * BLOCK, BLOCK), f32),
            pltpu.VMEM((2, blocks * slots + 1, BLOCK, HD), f32),
            pltpu.VMEM(chunk, f32),
            pltpu.VMEM(chunk, bf16),
            pltpu.VMEM(chunk, bf16),
            pltpu.VMEM(chunk, bf16),
            pltpu.VMEM(chunk, bf16),
        ] + [pltpu.VMEM((blocks, BLOCK, wide), bf16)] * 4 + [
            pltpu.SMEM((blocks, window_blocks), jnp.int32),
        ] + [dma((kv_heads, 2))] * 3 + [dma((kv_heads,))] * 8,
        compiler_params=pltpu.CompilerParams(
            collective_id=0, has_side_effects=True, vmem_limit_bytes=56 * 1024 * 1024
        ),
        cost_estimate=pl.CostEstimate(
            flops=12 * rows * wide * slots * BLOCK,
            bytes_accessed=8 * rows * (wide + slim),
            transcendentals=rows * (wide // HD) * slots * BLOCK,
        ),
    )(
        block_lists, doc_starts, shaped(keys), shaped(values), shaped(queries), shaped(out_grad),
    )
    results = pl.pallas_call(
        copy_kernel,
        out_shape=tuple(jax.ShapeDtypeStruct(result.shape, bf16) for result in results),
        in_specs=[hbm] * 4,
        out_specs=[hbm] * 4,
        scratch_shapes=[dma((4, blocks))],
        compiler_params=pltpu.CompilerParams(vmem_limit_bytes=56 * 1024 * 1024),
    )(*results)
    return tuple(result.reshape(rows, result.shape[2]) for result in results)


def solution(mesh):
    both = P(("grp", "ctx"), None)
    return jax.shard_map(
        functools.partial(per_device, mesh.shape["ctx"]),
        mesh=mesh,
        in_specs=(both, both, both, both, P("grp"), both),
        out_specs=(both, both, both, both),
        check_vma=False,
    )
```

```python
import functools

import jax
import jax.numpy as jnp
from jax import lax
from jax.experimental import pallas as pl
from jax.experimental.pallas import tpu as pltpu
from jax.sharding import PartitionSpec as P

HD = 128
BLOCK = 128
R_DEV = 2
MESH = pl.DeviceIdType.MESH
FAR = 1 << 30


def kernel(
    n, blocks, slots, kv_heads, groups,
    lists_ref, starts_ref, key_hbm, value_hbm, query_hbm, grad_hbm,
    out_hbm, dquery_hbm, dkey_ref, dvalue_ref,
    window, current, turned, bias, parts, own, send_a, send_b, take_a, take_b,
    query_buf, grad_buf, out_buf, dquery_buf, inverse,
    local_sem, load_sem, store_sem,
    a_send, a_recv, b_send, b_recv, ga_send, ga_recv, gb_send, gb_recv,
):
    me = lax.axis_index("ctx")
    odd = lax.rem(me, 2) == 1
    even = jnp.logical_not(odd)
    partner = me + 1 - 2 * lax.rem(me, 2)
    ahead = lax.rem(me + 2, n)
    behind = lax.rem(me + n - 2, n)
    here = pl.ds(2 * blocks, blocks)
    near = pl.ds(blocks, blocks)
    far = pl.ds(0, blocks)
    wide = groups * HD
    scaling = HD ** (-0.5)
    scale2 = scaling * 1.4426950408889634
    window_base = (me - R_DEV) * blocks

    def local_copies(g):
        cols = pl.ds(pl.multiple_of(g * HD, HD), HD)
        return [
            pltpu.make_async_copy(
                ref.at[:, :, cols], window.at[g, kind, here], local_sem.at[g, kind]
            )
            for kind, ref in enumerate((key_hbm, value_hbm))
        ]

    def loads(g):
        cols = pl.ds(pl.multiple_of(g * wide, wide), wide)
        return [
            pltpu.make_async_copy(ref.at[:, :, cols], buf.at[:, :, cols], load_sem.at[g, kind])
            for kind, (ref, buf) in enumerate(((query_hbm, query_buf), (grad_hbm, grad_buf)))
        ]

    def stores(g):
        cols = pl.ds(pl.multiple_of(g * wide, wide), wide)
        return [
            pltpu.make_async_copy(buf.at[:, :, cols], ref.at[:, :, cols], store_sem.at[g, kind])
            for kind, (ref, buf) in enumerate(((out_hbm, out_buf), (dquery_hbm, dquery_buf)))
        ]

    def remote(src, dst, send, recv, target):
        return pltpu.make_async_remote_copy(
            src_ref=src, dst_ref=dst, send_sem=send, recv_sem=recv,
            device_id={"ctx": target}, device_id_type=MESH,
        )

    def copy_a(g):
        return remote(
            window.at[g, :, here], window.at[g, :, far], a_send.at[g], a_recv.at[g], ahead
        )

    def copy_b(g, source):
        return remote(
            window.at[g, :, source], window.at[g, :, near], b_send.at[g], b_recv.at[g], partner
        )

    def grad_a(g):
        return remote(send_a.at[g], take_a.at[g], ga_send.at[g], ga_recv.at[g], behind)

    def grad_b(g):
        return remote(send_b.at[g], take_b.at[g], gb_send.at[g], gb_recv.at[g], partner)

    barrier = pltpu.get_barrier_semaphore()
    for other in (ahead, behind, partner):
        pl.semaphore_signal(barrier, inc=1, device_id={"ctx": other}, device_id_type=MESH)
    for g in range(kv_heads):
        for copy in local_copies(g):
            copy.start()
    for g in range(kv_heads):
        for copy in loads(g):
            copy.start()
    pl.semaphore_wait(barrier, 3)
    for g in range(kv_heads):
        for copy in local_copies(g):
            copy.wait()
        if g == 0:
            copy_a(g).start()

        @pl.when(even)
        def _():
            copy_b(g, here).start()

    parts[:, blocks * slots] = jnp.zeros((2, BLOCK, HD), jnp.float32)
    for b in range(blocks):
        for w in range((R_DEV + 1) * blocks):
            found = jnp.int32(blocks * slots)
            for s in range(slots):
                found = jnp.where(lists_ref[b, s] == window_base + w, b * slots + s, found)
            inverse[b, w] = jnp.where(window_base + w >= 0, found, blocks * slots)
    first = me * (blocks * BLOCK)
    lanes = lax.broadcasted_iota(jnp.int32, (1, BLOCK), 1)
    rows = lax.broadcasted_iota(jnp.int32, (BLOCK, BLOCK), 0)
    for b in range(blocks):
        pos = first + b * BLOCK + lanes
        low = jnp.zeros_like(pos)
        for d in range(starts_ref.shape[0]):
            start = starts_ref[d]
            low = jnp.maximum(low, jnp.where(start <= pos, start, 0))
        for s in range(slots):
            entry = lists_ref[b, s]
            at = jnp.where(entry >= 0, entry * BLOCK, FAR) + rows
            keep = jnp.logical_and(at <= pos, at >= low)
            bias[b, pl.ds(s * BLOCK, BLOCK), :] = jnp.where(keep, 0.0, -1e30)
    copy_a(0).wait_send()
    copy_a(1).start()

    def arrive(g):
        copy_a(g).wait_recv()

        @pl.when(odd)
        def _():
            copy_b(g, far).start()

    def forward_grad(g):
        grad_b(g).wait_recv()
        send_a[g] = (
            send_a[g].astype(jnp.float32) + take_b[g].astype(jnp.float32)
        ).astype(jnp.bfloat16)
        grad_a(g).start()

    def attend(g, b):
        cols = pl.ds(pl.multiple_of(g * (groups * HD), groups * HD), groups * HD)
        picks = []
        for s in range(slots):
            entry = lists_ref[b, s]
            spot = jnp.where(entry >= 0, entry - window_base, R_DEV * blocks)
            picks.append(jnp.clip(spot, 0, (R_DEV + 1) * blocks - 1))
        keys = jnp.concatenate([current[0, w] for w in picks], axis=0)
        values = jnp.concatenate([current[1, w] for w in picks], axis=0)
        keys_t = jnp.concatenate([turned[0, w] for w in picks], axis=1)
        values_t = jnp.concatenate([turned[1, w] for w in picks], axis=1)
        query_all = query_buf[b, :, cols]
        grad_all = grad_buf[b, :, cols]
        mask = jnp.concatenate([bias[b]] * groups, axis=1)
        query = jnp.concatenate(
            [query_all[:, j * HD:(j + 1) * HD] for j in range(groups)], axis=0
        )
        grad = jnp.concatenate([grad_all[:, j * HD:(j + 1) * HD] for j in range(groups)], axis=0)
        grad_t = jnp.concatenate(
            [grad_all[:, j * HD:(j + 1) * HD].T for j in range(groups)], axis=1
        )
        nt = (((1,), (1,)), ((), ()))
        scores = lax.dot_general(keys, query, nt, preferred_element_type=jnp.float32)
        dprobs = jnp.dot(values, grad_t, preferred_element_type=jnp.float32)
        scores = scores * scale2 + mask
        top = jnp.max(scores, axis=0, keepdims=True)
        probs = jnp.exp2(scores - top)
        probs = probs * (1.0 / jnp.sum(probs, axis=0, keepdims=True))
        low = probs.astype(jnp.bfloat16)
        out_t = jnp.dot(values_t, low, preferred_element_type=jnp.float32).astype(jnp.bfloat16)
        delta = jnp.sum(
            out_t.astype(jnp.float32) * grad_t.astype(jnp.float32), axis=0, keepdims=True
        )
        dscores = (probs * (dprobs - delta)).astype(jnp.bfloat16)
        dvalues = jnp.dot(low, grad, preferred_element_type=jnp.float32)
        dquery_t = (
            jnp.dot(keys_t, dscores, preferred_element_type=jnp.float32) * scaling
        ).astype(jnp.bfloat16)
        dkeys = jnp.dot(dscores, query, preferred_element_type=jnp.float32)
        for j in range(groups):
            spot = pl.ds(pl.multiple_of(g * wide + j * HD, HD), HD)
            out_buf[b, :, spot] = out_t[:, j * BLOCK:(j + 1) * BLOCK].T
            dquery_buf[b, :, spot] = dquery_t[:, j * BLOCK:(j + 1) * BLOCK].T
        parts[0, pl.ds(b * slots, slots)] = (dkeys * scaling).reshape(slots, BLOCK, HD)
        parts[1, pl.ds(b * slots, slots)] = dvalues.reshape(slots, BLOCK, HD)

    def head(g, _):
        copy_b(g, here).wait_recv()
        for copy in loads(g):
            copy.wait()
        for kind in range(2):
            for w in range((R_DEV + 1) * blocks):
                tile = window[g, kind, w]
                current[kind, w] = tile
                turned[kind, w] = tile.T

        def block(b, _):
            @pl.when(jnp.logical_and(b == 1, g < kv_heads - 2))
            def _():
                copy_a(g + 1).wait_send()
                copy_a(g + 2).start()

            @pl.when(jnp.logical_and(b == 1, jnp.logical_and(g > 0, odd)))
            def _():
                forward_grad(g - 1)

            @pl.when(jnp.logical_and(b == blocks - 1, g < kv_heads - 1))
            def _():
                arrive(g + 1)

            attend(g, b)
            return 0

        lax.fori_loop(0, blocks, block, 0)
        for kind in range(2):
            for w in range(blocks, 2 * blocks):
                total = parts[kind, inverse[0, w]]
                for b in range(1, blocks):
                    total = total + parts[kind, inverse[b, w]]
                send_b[g, kind, w - blocks] = total.astype(jnp.bfloat16)
        grad_b(g).start()
        for kind in range(2):
            for w in range(blocks):
                total = parts[kind, inverse[0, w]]
                for b in range(1, blocks):
                    total = total + parts[kind, inverse[b, w]]
                send_a[g, kind, w] = total.astype(jnp.bfloat16)

        @pl.when(even)
        def _():
            grad_a(g).start()

        for copy in stores(g):
            copy.start()
        for kind in range(2):
            for j in range(blocks):
                total = parts[kind, j * slots]
                for b in range(j + 1, blocks):
                    total = total + parts[kind, inverse[b, 2 * blocks + j]]
                own[g, kind, j] = total
        return 0

    arrive(0)
    lax.fori_loop(0, kv_heads, head, 0)

    @pl.when(odd)
    def _():
        forward_grad(kv_heads - 1)

    for g in range(kv_heads):
        @pl.when(even)
        def _():
            grad_b(g).wait_recv()
            own[g] = own[g] + take_b[g].astype(jnp.float32)

        grad_a(g).wait_recv()
        cols = pl.ds(g * HD, HD)
        for kind, ref in enumerate((dkey_ref, dvalue_ref)):
            ref[:, :, cols] = (own[g, kind] + take_a[g, kind].astype(jnp.float32)).astype(
                jnp.bfloat16
            )
    copy_a(kv_heads - 1).wait_send()
    for g in range(kv_heads):
        @pl.when(even)
        def _():
            copy_b(g, here).wait_send()

        @pl.when(odd)
        def _():
            copy_b(g, far).wait_send()

        grad_a(g).wait_send()
        grad_b(g).wait_send()
        for copy in stores(g):
            copy.wait()


def copy_kernel(*refs):
    for source, result in zip(refs[:4], refs[4:]):
        result[...] = source[...]


def per_device(n, queries, keys, values, out_grad, doc_starts, block_lists):
    blocks, slots = block_lists.shape
    rows = queries.shape[0]
    kv_heads = keys.shape[1] // HD
    groups = queries.shape[1] // keys.shape[1]
    window_blocks = (R_DEV + 1) * blocks
    wide, slim = queries.shape[1], keys.shape[1]

    def shaped(array):
        return array.reshape(blocks, BLOCK, array.shape[1])

    smem = pl.BlockSpec(memory_space=pltpu.SMEM)
    vmem = pl.BlockSpec(memory_space=pltpu.VMEM)
    hbm = pl.BlockSpec(memory_space=pl.ANY)
    bf16, f32 = jnp.bfloat16, jnp.float32
    chunk = (kv_heads, 2, blocks, BLOCK, HD)
    dma = pltpu.SemaphoreType.DMA
    results = pl.pallas_call(
        functools.partial(kernel, n, blocks, slots, kv_heads, groups),
        out_shape=(
            jax.ShapeDtypeStruct((blocks, BLOCK, wide), bf16),
            jax.ShapeDtypeStruct((blocks, BLOCK, wide), bf16),
            jax.ShapeDtypeStruct((blocks, BLOCK, slim), bf16),
            jax.ShapeDtypeStruct((blocks, BLOCK, slim), bf16),
        ),
        in_specs=[smem] * 2 + [hbm] * 4,
        out_specs=[hbm] * 2 + [vmem] * 2,
        scratch_shapes=[
            pltpu.VMEM((kv_heads, 2, window_blocks, BLOCK, HD), bf16),
            pltpu.VMEM((2, window_blocks, BLOCK, HD), bf16),
            pltpu.VMEM((2, window_blocks, BLOCK, HD), bf16),
            pltpu.VMEM((blocks, slots * BLOCK, BLOCK), f32),
            pltpu.VMEM((2, blocks * slots + 1, BLOCK, HD), f32),
            pltpu.VMEM(chunk, f32),
            pltpu.VMEM(chunk, bf16),
            pltpu.VMEM(chunk, bf16),
            pltpu.VMEM(chunk, bf16),
            pltpu.VMEM(chunk, bf16),
        ] + [pltpu.VMEM((blocks, BLOCK, wide), bf16)] * 4 + [
            pltpu.SMEM((blocks, window_blocks), jnp.int32),
        ] + [dma((kv_heads, 2))] * 3 + [dma((kv_heads,))] * 8,
        compiler_params=pltpu.CompilerParams(
            collective_id=0, has_side_effects=True, vmem_limit_bytes=56 * 1024 * 1024
        ),
        cost_estimate=pl.CostEstimate(
            flops=12 * rows * wide * slots * BLOCK,
            bytes_accessed=8 * rows * (wide + slim),
            transcendentals=rows * (wide // HD) * slots * BLOCK,
        ),
    )(
        block_lists, doc_starts, shaped(keys), shaped(values), shaped(queries), shaped(out_grad),
    )

    def half_block(result):
        return pl.BlockSpec((1, BLOCK // 2, result.shape[2]), lambda i: (i // 2, i % 2, 0))

    results = pl.pallas_call(
        copy_kernel,
        out_shape=tuple(jax.ShapeDtypeStruct(result.shape, bf16) for result in results),
        grid=(rows // (BLOCK // 2),),
        in_specs=[half_block(result) for result in results],
        out_specs=[half_block(result) for result in results],
        compiler_params=pltpu.CompilerParams(vmem_limit_bytes=56 * 1024 * 1024),
    )(*results)
    return tuple(result.reshape(rows, result.shape[2]) for result in results)


def solution(mesh):
    both = P(("grp", "ctx"), None)
    return jax.shard_map(
        functools.partial(per_device, mesh.shape["ctx"]),
        mesh=mesh,
        in_specs=(both, both, both, both, P("grp"), both),
        out_specs=(both, both, both, both),
        check_vma=False,
    )
```
